256 devices in a mesh: sub: 4 (over y_lo, core), prow: 8 (over z), pcol: 8 (over y_hi, x).
Axes of the slice: x: 4, y: 4 (y_hi: 2, y_lo: 2; y = y_hi * 2 + y_lo), z: 8, core: 2. Of those that a mesh axis runs over, the one named last changes fastest.
Arguments:
- child_front: float32 [4, 6656, 6656], P('sub', 'prow', 'pcol')
- child_order: int32 [4, 512], P('sub'), may hold values from 0 to 511, as said below
- parent_front: float32 [8704, 8704], P('prow', ('sub', 'pcol'))
- parent_order: int32 [512], replicated, may hold values from 0 to 511, as said below
- row_map: int32 [4, 48], P('sub', 'prow'), may hold values from 0 to 63, as said below
- col_map: int32 [4, 48], P('sub', 'pcol'), may hold values from 0 to 63, as said below
Outputs:
- child_lower: float32 [4, 6144, 512], P('sub', 'prow', 'pcol')
- parent_lower: float32 [8192, 512], P('prow', ('sub', 'pcol'))
- parent_schur: float32 [8192, 8192], P('prow', ('sub', 'pcol'))
The draws below stay inside these ranges and needn't reach their ends.
Inputs may be any that keep to these rules, and one draw needn't show every extreme that they name: `child_order`: each row is a permutation of 0 to 511. `parent_order`: A permutation of 0 to 511. Within one child the values are distinct; trailing row block i of a child, held by process row i // 6, goes to a parent trailing row block held by the same process row, that is row_map[s, i] // 8 == i // 6. Within one child the values are distinct; child trailing column block j, held by process column j // 6, goes to a parent trailing column block held by a parent column device whose pcol index is the same: (col_map[s, j] // 2) % 8 == j // 6.
All inputs are finite; a program needn't handle non-finite values.
Results may differ from the reference program's by a relative error of at most 0.0001.
Values sent between devices are 32-bit elements; how exact they have to be, the bound alone decides.
No kernel may reach another device: no remote copies, remote signals or barrier semaphores. Data moves between devices by JAX's collectives and lax.ppermute only.
A program may use at most 128 MiB of HBM per device.

```python
import jax
import jax.numpy as jnp
from jax import lax

NC = 6656
NP = 8704
PB = 512
BLK = 128
NS_STEPS = 5
NSUB = 4
PROWS = 8
PCOLS = 8
CPR = 64
CPC = 64
PPC = 16
NCR = 832
NCC = 832
NPRD = 1088
NPCD = 272
CRB = 6
CCB = 6
PRB = 8
PCB = 2


def order_rows(key, count, salt):
    keys = jax.random.split(jax.random.fold_in(key, salt), count)
    return jax.vmap(lambda one_key: jax.random.permutation(one_key, PB))(keys).astype(jnp.int32)


def pivot_list_drawn(per_dev, piv_per):
    steps = jnp.arange(PB, dtype=jnp.int32)
    return steps // piv_per * per_dev + steps % piv_per


def build_front(base, diag_key, pivot_seq, rows_dev, cols_dev, row_piv, col_piv):
    row_count, col_count = base.shape
    row_is = jnp.arange(row_count) % rows_dev < row_piv
    col_is = jnp.arange(col_count) % cols_dev < col_piv
    scale = jnp.where(row_is[:, None] & col_is[None, :], PB ** (-0.5), 1.0)
    values = base * scale
    diag_vals = jax.random.uniform(diag_key, (PB,), jnp.float32, 4.0, 5.0)
    row_idx = pivot_list_drawn(rows_dev, row_piv)
    col_idx = pivot_list_drawn(cols_dev, col_piv)[pivot_seq]
    return values.at[row_idx, col_idx].add(diag_vals)


def draw_child_order(key, part):
    return order_rows(key, NSUB, 71)


def draw_parent_order(key, part):
    return order_rows(key, 1, 83)[0]


def draw_child_front(key, part):
    sequences = order_rows(key, NSUB, 71)
    key = jax.random.fold_in(key, 1)
    base_key, diag_key = jax.random.split(key)
    base = jax.random.normal(base_key, (NSUB, NC, NC), jnp.float32)
    diag_keys = jax.random.split(diag_key, NSUB)
    return jax.vmap(lambda one_base, one_key, one_seq: build_front(one_base, one_key, one_seq, NCR, NCC, CPR, CPC))(base, diag_keys, sequences)


def draw_parent_front(key, part):
    sequence = order_rows(key, 1, 83)[0]
    key = jax.random.fold_in(key, 2)
    base_key, diag_key = jax.random.split(key)
    base = jax.random.normal(base_key, (NP, NP), jnp.float32)
    return build_front(base, diag_key, sequence, NPRD, NPCD, CPR, PPC)


def pick_blocks(one_key, pool, count):
    first_key, second_key = jax.random.split(one_key)
    middle = jax.random.permutation(first_key, pool - 2)[:count - 2] + 1
    chosen = jnp.concatenate([jnp.array([0], jnp.int32), middle.astype(jnp.int32), jnp.array([pool - 1], jnp.int32)]).astype(jnp.int32)
    return chosen[jax.random.permutation(second_key, count)]


def draw_row_map(key, part):
    key = jax.random.fold_in(key, 5)
    keys = jax.random.split(key, NSUB * PROWS)
    groups = jnp.arange(NSUB * PROWS, dtype=jnp.int32)

    def one_group(one_key, group):
        return pick_blocks(one_key, PRB, CRB) + group % PROWS * PRB
    return jax.vmap(one_group)(keys, groups).reshape(NSUB, PROWS * CRB).astype(jnp.int32)


def draw_col_map(key, part):
    key = jax.random.fold_in(key, 6)
    keys = jax.random.split(key, NSUB * PCOLS)
    groups = jnp.arange(NSUB * PCOLS, dtype=jnp.int32)

    def one_group(one_key, group):
        chosen = pick_blocks(one_key, NSUB * PCB, CCB)
        column = group % PCOLS
        return (chosen // PCB * PCOLS + column) * PCB + chosen % PCB
    return jax.vmap(one_group)(keys, groups).reshape(NSUB, PCOLS * CCB).astype(jnp.int32)


def setup_inputs(seed: int = 0) -> dict:
    splits = jax.random.split(jax.random.key(seed), 7)
    child_front = draw_child_front(jax.random.fold_in(splits[6], 71), 0)
    child_order = draw_child_order(jax.random.fold_in(splits[6], 71), 0)
    parent_front = draw_parent_front(jax.random.fold_in(splits[6], 71), 0)
    parent_order = draw_parent_order(jax.random.fold_in(splits[6], 71), 0)
    row_map = draw_row_map(jax.random.fold_in(splits[6], 71), 0)
    col_map = draw_col_map(jax.random.fold_in(splits[6], 71), 0)
    return dict(child_front=child_front, child_order=child_order, parent_front=parent_front, parent_order=parent_order, row_map=row_map, col_map=col_map)


HIGH = lax.Precision.HIGHEST


def pivot_list(per_dev, piv_per):
    steps = jnp.arange(PB, dtype=jnp.int32)
    return (steps // piv_per) * per_dev + steps % piv_per


def rest_list(total, per_dev, piv_per):
    groups = total // per_dev
    starts = jnp.arange(groups, dtype=jnp.int32)[:, None] * per_dev + piv_per
    return (starts + jnp.arange(per_dev - piv_per, dtype=jnp.int32)[None, :]).reshape(-1)


def inverse_of(panel_block):
    eye = jnp.eye(PB, dtype=jnp.float32)
    estimate = jnp.diag(1.0 / jnp.diagonal(panel_block))
    for sweep in range(NS_STEPS):
        inner = 2.0 * eye - jnp.dot(panel_block, estimate, precision=HIGH, preferred_element_type=jnp.float32)
        estimate = jnp.dot(estimate, inner, precision=HIGH, preferred_element_type=jnp.float32)
    return estimate


def panel_step(front_block, pivot_seq, rows_dev, cols_dev, row_piv, col_piv):
    piv_rows = pivot_list(rows_dev, row_piv)
    piv_cols = pivot_list(cols_dev, col_piv)
    rest_rows = rest_list(front_block.shape[0], rows_dev, row_piv)
    rest_cols = rest_list(front_block.shape[1], cols_dev, col_piv)
    panel_block = front_block[piv_rows][:, piv_cols][:, pivot_seq]
    left_cols = front_block[rest_rows][:, piv_cols][:, pivot_seq]
    upper_rows = front_block[piv_rows][:, rest_cols]
    trailing = front_block[rest_rows][:, rest_cols]
    lower_part = jnp.dot(left_cols, inverse_of(panel_block), precision=HIGH, preferred_element_type=jnp.float32)
    return lower_part, trailing, upper_rows


def one_hot(values, count):
    return (values[None, :] == jnp.arange(count, dtype=jnp.int32)[:, None]).astype(jnp.float32)


def place_blocks(rows_hot, piece, cols_hot):
    p_count, j_count = rows_hot.shape
    q_count, k_count = cols_hot.shape
    blocks = piece.reshape(j_count, BLK, k_count, BLK)
    placed = jnp.einsum("pj,jakb,qk->paqb", rows_hot, blocks, cols_hot, precision=HIGH)
    return placed.reshape(p_count * BLK, q_count * BLK)


def reference(child_front, child_order, parent_front, parent_order, row_map, col_map):
    parent_blocks = (NP - PB) // BLK
    contribution = jnp.zeros((NP - PB, NP - PB), jnp.float32)
    lowers = []
    for child in range(NSUB):
        lower_part, trailing, upper_rows = panel_step(child_front[child], child_order[child], NCR, NCC, CPR, CPC)
        schur = trailing - jnp.dot(lower_part, upper_rows, precision=HIGH, preferred_element_type=jnp.float32)
        contribution = contribution + place_blocks(one_hot(row_map[child], parent_blocks), schur, one_hot(col_map[child], parent_blocks))
        lowers.append(lower_part)
    parent_lower, parent_trail, parent_upper = panel_step(parent_front, parent_order, NPRD, NPCD, CPR, PPC)
    parent_schur = (parent_trail + contribution) - jnp.dot(parent_lower, parent_upper, precision=HIGH, preferred_element_type=jnp.float32)
    return jnp.stack(lowers), parent_lower, parent_schur
```

```python
import functools

import jax
import jax.numpy as jnp
from jax import lax
from jax.experimental import pallas as pl
from jax.experimental.pallas import tpu as pltpu
from jax.sharding import PartitionSpec as P

PB = 512
BLK = 128

HIGH = lax.Precision.HIGH
HIGHEST = lax.Precision.HIGHEST
F32 = jnp.float32


def dot(a, b, precision=HIGH):
    return jnp.dot(a, b, precision=precision, preferred_element_type=F32)


def dot_t(a, b, precision=HIGH):
    return lax.dot_general(
        a, b, (((0,), (0,)), ((), ())), precision=precision, preferred_element_type=F32
    )


def flip(axis, size, mask):
    return functools.partial(
        lax.ppermute, axis_name=axis, perm=[(i, i ^ mask) for i in range(size)]
    )


def x_step(value, step):
    pairs = [(i, i // 4 * 4 + (i % 4 + step) % 4) for i in range(8)]
    return lax.ppermute(value, "pcol", pairs)


def x_gather(own):
    half = own.shape[0] // 2
    below = x_step(own, 1)
    above = x_step(own, -1)
    far_low = x_step(below[:half], 1)
    far_high = x_step(above[half:], -1)
    return jnp.concatenate([own, below, far_low, far_high, above], 0)


def inverse_slots(targets, count):
    hit = targets[None, :] == jnp.arange(count, dtype=jnp.int32)[:, None]
    source = jnp.sum(
        jnp.where(hit, jnp.arange(targets.shape[0], dtype=jnp.int32)[None, :], 0), axis=1
    )
    return source.astype(jnp.int32), jnp.any(hit, axis=1).astype(jnp.int32)


def place_cols_kernel(src, valid, x_ref, o_ref):
    live = valid[pl.program_id(0)] > 0

    @pl.when(live)
    def _():
        o_ref[...] = x_ref[...]

    @pl.when(jnp.logical_not(live))
    def _():
        o_ref[...] = jnp.zeros_like(o_ref)


def place_cols(value, src, valid):
    rows = value.shape[0]
    count = src.shape[0]
    return pl.pallas_call(
        place_cols_kernel,
        out_shape=jax.ShapeDtypeStruct((rows, count * BLK), F32),
        grid_spec=pltpu.PrefetchScalarGridSpec(
            num_scalar_prefetch=2,
            grid=(count,),
            in_specs=[pl.BlockSpec((rows, BLK), lambda p, src, valid: (0, src[p]))],
            out_specs=pl.BlockSpec((rows, BLK), lambda p, src, valid: (0, p)),
        ),
        cost_estimate=pl.CostEstimate(
            flops=0, bytes_accessed=8 * rows * count * BLK, transcendentals=0
        ),
    )(src, valid, value)


def place_both_kernel(rsrc, rvalid, csrc, cvalid, x_ref, o_ref):
    row_live = rvalid[pl.program_id(0)]
    for q in range(o_ref.shape[1] // BLK):
        live = row_live * cvalid[q] > 0
        start = pl.multiple_of(csrc[q] * BLK, BLK)
        block = x_ref[:, pl.ds(start, BLK)]
        o_ref[:, q * BLK : (q + 1) * BLK] = jnp.where(live, block, 0.0)


def place_both(value, rsrc, rvalid, csrc, cvalid):
    rcount, ccount = rsrc.shape[0], csrc.shape[0]
    width = value.shape[1]
    return pl.pallas_call(
        place_both_kernel,
        out_shape=jax.ShapeDtypeStruct((rcount * BLK, ccount * BLK), F32),
        grid_spec=pltpu.PrefetchScalarGridSpec(
            num_scalar_prefetch=4,
            grid=(rcount,),
            in_specs=[pl.BlockSpec((BLK, width), lambda p, a, b, c, d: (a[p], 0))],
            out_specs=pl.BlockSpec((BLK, ccount * BLK), lambda p, a, b, c, d: (p, 0)),
        ),
        cost_estimate=pl.CostEstimate(
            flops=0, bytes_accessed=8 * rcount * ccount * BLK * BLK, transcendentals=0
        ),
    )(rsrc, rvalid, csrc, cvalid, value)


def picks(positions):
    return positions[:, None] == jnp.arange(PB, dtype=jnp.int32)[None, :]


def series(panel_t, hot):
    diag = jnp.sum(jnp.where(hot, panel_t.T, 0.0), axis=1)
    inv_diag = 1.0 / diag
    eye = jnp.eye(PB, dtype=F32)
    error = eye - dot(hot.astype(F32), panel_t, HIGHEST) * inv_diag[:, None]
    total = eye + error
    power = error
    for _ in range(4):
        power = dot(power, power)
        total = total + dot(power, total)
    return total, inv_diag


def body(child_front, child_order, parent_front, parent_order, row_map, col_map):
    sub = lax.axis_index("sub")
    pcol = lax.axis_index("pcol")
    core_flip = flip("sub", 4, 1)
    ylo_flip = flip("sub", 4, 2)
    yhi_flip = flip("pcol", 8, 4)
    front = child_front[0]
    n = 64
    pp = 16
    parent_t = parent_front.T

    uppers = lax.all_gather(
        jnp.concatenate([front[:n, n:], parent_front[:n, pp:]], 1), "prow", axis=0, tiled=True
    )

    piece = jnp.concatenate(
        [front[:n, :n], parent_front[:n, :pp], jnp.zeros((n, BLK - n - pp), F32)], 1
    )
    pieces = lax.all_to_all(
        jnp.broadcast_to(piece[None], (8, n, BLK)), "prow", 0, 0, tiled=True
    )
    pieces_t = pieces.reshape(8 * n, BLK).T

    left_t = front[n:, :n].T
    left_two = jnp.concatenate([left_t, yhi_flip(left_t)], 0)
    left_all = x_gather(left_two)

    panel_own = pieces_t[:n]
    panel_two = jnp.concatenate([panel_own, yhi_flip(panel_own)], 0)
    panel_t = lax.all_gather(
        panel_two, "pcol", axis=0, tiled=True, axis_index_groups=[[0, 1, 2, 3], [4, 5, 6, 7]]
    )

    order = child_order[0]
    owner, offset = order // n, order % n
    yhi, x = pcol // 4, pcol % 4
    yhi_rel = (owner // 4) ^ yhi
    x_rel = (x - owner % 4) % 4
    hot = picks((owner % 4) * 2 * n + yhi_rel * n + offset)
    hot_left = picks(x_rel * 2 * n + yhi_rel * n + offset)

    rsrc, rvalid = inverse_slots(row_map[0] % 8, 8)
    col_vals = col_map[0]
    target = ((col_vals // 16) ^ sub) * 2 + col_vals % 2
    csrc, cvalid = inverse_slots(target, 8)
    trail = place_both(front[n:, n:], rsrc, rvalid, csrc, cvalid)
    left_placed = place_cols(left_all, rsrc, rvalid)
    left_sorted = dot(hot_left.astype(F32), left_placed, HIGHEST)
    upper = place_cols(uppers[:, :768], csrc, cvalid)

    total, inv_diag = series(panel_t, hot)
    lower_t = dot(total, left_sorted * inv_diag[:, None])

    def term(slot):
        cols = slice(slot * 256, (slot + 1) * 256)
        return trail[:, cols] - dot_t(lower_t, upper[:, cols])

    over = core_flip(term(3))
    far = ylo_flip(term(2) + over)
    near = core_flip(term(1))
    mine = term(0) + near

    own_rows = lax.dynamic_slice_in_dim(lower_t, pcol * n, n, 0)
    own_lower = jnp.concatenate(
        [
            lax.dynamic_slice_in_dim(own_rows, (row_map[0, j] % 8) * BLK, BLK, 1)
            for j in range(6)
        ],
        1,
    ).T

    parent_own = jnp.concatenate([pieces_t[n : n + pp], parent_t[:pp, n:]], 1)
    parent_two = jnp.concatenate([parent_own, yhi_flip(parent_own)], 0)
    parent_four = jnp.concatenate([parent_two, ylo_flip(parent_two)], 0)
    parent_half = x_gather(parent_four)
    parent_all = jnp.concatenate([parent_half, core_flip(parent_half)], 0)
    powner, poffset = parent_order // pp, parent_order % pp
    psub, ppcol = powner // 8, powner % 8
    slot = (psub % 2) ^ (sub % 2)
    slot = slot * 4 + (x - ppcol % 4) % 4
    slot = slot * 2 + ((psub // 2) ^ (sub // 2))
    slot = slot * 2 + ((ppcol // 4) ^ yhi)
    phot = picks(slot * pp + poffset)
    ptotal, pinv_diag = series(parent_all[:, :PB], phot)
    pleft = dot(phot.astype(F32), parent_all[:, PB:], HIGHEST) * pinv_diag[:, None]
    plower_t = dot(ptotal, pleft)
    parent_lower = lax.dynamic_slice_in_dim(plower_t, (sub * 8 + pcol) * pp, pp, 0).T
    base = parent_t[pp:, n:].T - dot_t(plower_t, uppers[:, 768:])
    parent_schur = base + mine + far
    return (own_lower[None], parent_lower, parent_schur)


def solution(mesh):
    placed = (
        P("sub", "prow", "pcol"),
        P("sub", None),
        P("prow", ("sub", "pcol")),
        P(),
        P("sub", "prow"),
        P("sub", "pcol"),
    )
    return jax.shard_map(
        body,
        mesh=mesh,
        in_specs=placed,
        out_specs=(
            P("sub", "prow", "pcol"),
            P("prow", ("sub", "pcol")),
            P("prow", ("sub", "pcol")),
        ),
        check_vma=False,
    )
```

```python
import functools

import jax
import jax.numpy as jnp
from jax import lax
from jax.experimental import pallas as pl
from jax.experimental.pallas import tpu as pltpu
from jax.sharding import PartitionSpec as P

PB = 512
BLK = 128
N = 64
PP = 16
CT = 768
PT = 1024
F32 = jnp.float32
BF16 = jnp.bfloat16
VMEM = pl.BlockSpec(memory_space=pltpu.VMEM)
ANY = pl.BlockSpec(memory_space=pl.ANY)
SMEM = pl.BlockSpec(memory_space=pltpu.SMEM)


def flip(axis, size, mask):
    return functools.partial(
        lax.ppermute, axis_name=axis, perm=[(i, i ^ mask) for i in range(size)]
    )


core_flip = flip("sub", 4, 1)
ylo_flip = flip("sub", 4, 2)
yhi_flip = flip("pcol", 8, 4)


def x_step(value, step):
    pairs = [(i, i // 4 * 4 + (i % 4 + step) % 4) for i in range(8)]
    return lax.ppermute(value, "pcol", pairs)


def pcol_gather(copies):
    return lax.all_to_all(copies, "pcol", 0, 0, tiled=True)


def pcol_steps(own):
    flip_own = yhi_flip(own)
    below, above = x_step(own, 1), x_step(own, -1)
    below_flip, above_flip = x_step(flip_own, 1), x_step(flip_own, -1)
    far, far_flip = x_step(below, 1), x_step(above_flip, -1)
    return [own, flip_own, below, below_flip, far, far_flip, above, above_flip]


def z_step(value, step):
    return lax.ppermute(value, "prow", [(i, (i + step) % 8) for i in range(8)])


def call(kernel, outs, ins, scratch=(), flops=0, smem=0, parts=0, moved=None, limit=60):
    whole = len(ins) - smem - parts
    if moved is None:
        moved = sum(o.size * o.dtype.itemsize for o in list(outs) + list(ins))
    return pl.pallas_call(
        kernel,
        out_shape=tuple(outs),
        in_specs=[SMEM] * smem + [VMEM] * whole + [ANY] * parts,
        out_specs=tuple([VMEM] * len(outs)),
        scratch_shapes=list(scratch),
        compiler_params=pltpu.CompilerParams(vmem_limit_bytes=limit * 1024 * 1024),
        cost_estimate=pl.CostEstimate(flops=flops, bytes_accessed=moved, transcendentals=0),
    )(*ins)


def sds(*shape, dtype=F32):
    return jax.ShapeDtypeStruct(shape, dtype)


def split(value):
    high = value.astype(BF16)
    return high, (value - high.astype(F32)).astype(BF16)


def mm(a, b):
    return jnp.dot(a, b, preferred_element_type=F32)


def mm3(ah, al, bh, bl):
    return mm(ah, bh) + (mm(ah, bl) + mm(al, bh))


def select(hot, value):
    first = value.astype(BF16)
    rest = value - first.astype(F32)
    second = rest.astype(BF16)
    third = (rest - second.astype(F32)).astype(BF16)
    return mm(hot, first) + (mm(hot, second) + mm(hot, third))


def hot_rows(order, meta, held):
    sub, pcol = meta[0], meta[1]
    x, yhi = pcol & 3, pcol >> 2
    if held == "parent":
        owner = order >> 4
        pos = (((owner >> 3) ^ sub) & 1) * 2 + (((owner >> 4) ^ (sub >> 1)) & 1)
        pos = pos * 8 + ((x - owner) & 3) * 2 + (((owner >> 2) ^ yhi) & 1)
        pos = pos * PP + (order & (PP - 1))
    elif held == "left":
        owner = order >> 6
        pos = ((x - owner) & 3) * 2 * N + (((owner >> 2) ^ yhi) & 1) * N + (order & (N - 1))
    else:
        pos = order
    down = jnp.broadcast_to(pos.astype(F32), (BLK, PB)).T
    lanes = lax.broadcasted_iota(jnp.int32, (PB, BLK), 1)
    parts = []
    for c in range(PB // BLK):
        hit = down == (lanes + c * BLK).astype(F32)
        parts.append(jnp.where(hit, 1.0, 0.0).astype(BF16))
    return jnp.concatenate(parts, 1)


def series(panel_t, hot, ph, pw, th, tl, tf):
    eye = (
        lax.broadcasted_iota(jnp.int32, (PB, PB), 0) == lax.broadcasted_iota(jnp.int32, (PB, PB), 1)
    )
    picked = select(hot, panel_t)
    diag = jnp.sum(jnp.where(eye, picked, 0.0), axis=1, keepdims=True)
    inv_diag = 1.0 / diag
    error = jnp.where(eye, 1.0, 0.0) - picked * inv_diag
    ph[...], pw[...] = split(error)
    total = jnp.where(eye, 1.0, 0.0) + error
    tf[...] = total
    th[...], tl[...] = split(total)

    @pl.loop(0, 4)
    def _(_):
        h, w = split(mm3(ph[...], pw[...], ph[...], pw[...]))
        ph[...] = h
        pw[...] = w
        new = tf[...] + mm3(ph[...], pw[...], th[...], tl[...])
        tf[...] = new
        th[...], tl[...] = split(new)

    return inv_diag


SERIES_SCRATCH = [pltpu.VMEM((PB, PB), BF16)] * 4 + [pltpu.VMEM((PB, PB), F32)]
DMAS = lambda n: pltpu.SemaphoreType.DMA((n,))
SERIES_FLOPS = 2 * PB**3 * 27


def prep_kernel(front_rows, front_cols, parent_cols, parent_rows, piece, uppers, left_t):
    corner = front_rows[:, :N].T
    for z in range(8):
        piece[z, :32, :N] = corner[:32]
        piece[z, :32, N:] = corner[32:]
        piece[z, 32:, :N] = parent_cols[: PP // 2, :N]
        piece[z, 32:, N:] = parent_cols[PP // 2 : PP, :N]
    uppers[:, :CT] = front_rows[:, N:]
    uppers[:, CT:] = parent_cols[PP:, :N].T
    left_t[:, :CT] = front_cols[N:, :N].T
    for c in range(4):
        left_t[c * PP : (c + 1) * PP, CT:] = parent_rows[:, N + c * 256 : N + (c + 1) * 256]


def prep(front, parent_t):
    first = lambda i: (0, 0)
    return pl.pallas_call(
        prep_kernel,
        out_shape=(sds(8, 40, BLK), sds(N, PT), sds(N, CT + 256)),
        grid=(1,),
        in_specs=[
            pl.BlockSpec((N, CT + N), first),
            pl.BlockSpec((CT + N, BLK), first),
            pl.BlockSpec((PP + 256, BLK), first),
            pl.BlockSpec((PP, N + PT), first),
        ],
        out_specs=(
            pl.BlockSpec((8, 40, BLK), lambda i: (0, 0, 0)),
            pl.BlockSpec((N, PT), first),
            pl.BlockSpec((N, CT + 256), first),
        ),
        compiler_params=pltpu.CompilerParams(vmem_limit_bytes=60 * 1024 * 1024),
    )(front, front, parent_t, parent_t)


def mid_kernel(pieces, *refs):
    panel = refs[-1]
    for z in range(8):
        at = slice(z * N, (z + 1) * N)
        for i in range(8):
            panel[i, :32, at] = pieces[z, :32, :N]
            panel[i, 32:N, at] = pieces[z, :32, N:]
            panel[i, N : N + PP // 2, at] = pieces[z, 32:, :N]
            panel[i, N + PP // 2 :, at] = pieces[z, 32:, N:]


def x_fetch(dest, parts, sems):
    copies, start = [], 0
    for i, part in enumerate(parts):
        rows = pl.ds(start, part.shape[0])
        source = part.at[:, pl.ds(0, dest.shape[1])]
        copies.append(pltpu.make_async_copy(source, dest.at[rows, :], sems.at[i]))
        start += part.shape[0]
    return copies


def z_fetch(dest, cols, meta, parts, offset, sems):
    copies = []
    for i, part in enumerate(parts):
        owner = (meta[2] + (8 - i if i <= 4 else i - 4)) & 7
        rows = pl.ds(pl.multiple_of(owner * N, N), N)
        source = part.at[:, pl.ds(offset, cols)]
        copies.append(pltpu.make_async_copy(source, dest.at[rows, :], sems.at[i]))
    return copies


def begin(copies):
    for copy in copies:
        copy.start()


def finish(copies):
    for copy in copies:
        copy.wait()


def child_inverse_kernel(meta, order, blocks, *refs):
    sh, sl, inv, ph, pw, tf, panel, sems = refs[3:]
    copies = x_fetch(panel, [blocks.at[i, pl.ds(0, N), :] for i in range(8)], sems)
    begin(copies)
    hot = hot_rows(order[...], meta, "panel")
    finish(copies)
    inv[...] = series(panel[...], hot, ph, pw, sh, sl, tf)


def sources(targets, want):
    source, live = jnp.int32(0), jnp.int32(0)
    for j in range(6):
        hit = jnp.where(targets[j] == want, 1, 0).astype(jnp.int32)
        source += hit * j
        live += hit
    return source, live


def row_place(row_map, p):
    return sources([row_map[0, j] & 7 for j in range(6)], p)


def col_place(meta, col_map, q):
    values = [col_map[0, j] for j in range(6)]
    return sources([((v >> 4) ^ meta[0]) * 2 + (v & 1) for v in values], q)


def schur_kernel(meta, row_map, col_map, order, inv, *refs):
    left_parts, upper_parts, (sh_in, sl_in, front_in) = refs[:8], refs[8:16], refs[16:19]
    own_lower, outs = refs[20], refs[21:25]
    left, lower_t, upper, sh, sl, front, fetched = refs[25:]
    first = x_fetch(left, left_parts, fetched.at[pl.ds(0, 8)])
    second = [
        pltpu.make_async_copy(sh_in, sh, fetched.at[16]),
        pltpu.make_async_copy(sl_in, sl, fetched.at[17]),
    ]
    third = z_fetch(upper, CT, meta, upper_parts, 0, fetched.at[pl.ds(8, 8)])
    third.append(pltpu.make_async_copy(front_in.at[pl.ds(N, CT), :], front, fetched.at[18]))
    begin(first + second + third)
    hot = hot_rows(order[...], meta, "left")
    finish(first)
    high, low = split(select(hot, left[...]) * inv[...])
    finish(second)
    lower_t[...] = mm3(sh[...], sl[...], high, low)
    own_lower[...] = lower_t[pl.ds(pl.multiple_of(meta[1] * N, N), N), :]
    finish(third)
    uh, ul = split(upper[...])
    for i in range(3):
        lh, ll = split(lower_t[:, i * 256 : (i + 1) * 256].T)
        rows = slice(i * 256, (i + 1) * 256)
        front[rows, :CT] = front[rows, N:] - mm3(lh, ll, uh, ul)
    for slot, out in enumerate(outs):
        for b in range(2):
            csrc, clive = col_place(meta, col_map, slot * 2 + b)
            for p in range(8):
                rsrc, rlive = row_place(row_map, p)
                block = front[
                    pl.ds(pl.multiple_of(rsrc * BLK, BLK), BLK),
                    pl.ds(pl.multiple_of(csrc * BLK, BLK), BLK),
                ]
                here = (slice(p * BLK, (p + 1) * BLK), slice(b * BLK, (b + 1) * BLK))
                out[here] = jnp.where(rlive * clive > 0, block, 0.0)


def parent_rows_kernel(meta, blocks, *refs):
    parts, (out, panel, left, sems) = refs[:8], refs[8:]
    copies = [
        pltpu.make_async_copy(blocks.at[:, pl.ds(N, PP), :], panel, sems.at[8])
    ]
    for i, part in enumerate(parts):
        source = part.at[:, pl.ds(CT, 256)]
        copies.append(pltpu.make_async_copy(source, left.at[i], sems.at[i]))
    begin(copies)
    finish(copies)
    x, yhi = meta[1] & 3, meta[1] >> 2
    for i in range(8):
        owner = ((yhi ^ (i & 1)) * 4) + ((x - i // 2) & 3)
        rows = slice(i * PP, (i + 1) * PP)
        out[rows, :PB] = panel[owner]
        for c in range(4):
            at = slice(PB + c * 256, PB + (c + 1) * 256)
            out[rows, at] = left[i, c * PP : (c + 1) * PP, :]


def parent_kernel(meta, order, *refs):
    upper_parts, halves, tops, parent_t = refs[:8], refs[8:12], refs[12:14], refs[14]
    lower_out, out, ph, pw, th, tl, tf, whole, upper, near, zero, front, sems = refs[15:]
    first = x_fetch(whole, halves, sems.at[pl.ds(0, 4)])
    second = z_fetch(upper, 256, meta, upper_parts, CT, sems.at[pl.ds(4, 8)])
    second.append(pltpu.make_async_copy(tops[0], near, sems.at[12]))
    second.append(pltpu.make_async_copy(tops[1], zero, sems.at[13]))
    second.append(pltpu.make_async_copy(parent_t.at[pl.ds(PP, 256), :], front, sems.at[14]))
    begin(first + second)
    hot = hot_rows(order[...], meta, "parent")
    finish(first)
    inv = series(whole[:, :PB], hot, ph, pw, th, tl, tf)
    high, low = split(select(hot, whole[:, PB:]) * inv)
    whole[:, PB:] = mm3(th[...], tl[...], high, low)
    at = pl.multiple_of((meta[0] * 8 + meta[1]) * PP, PP)
    lower_out[...] = whole[pl.ds(at, PP), PB:]
    finish(second)
    uh, ul = split(upper[...])
    for p in range(4):
        h, w = split(whole[:, PB + p * 256 : PB + (p + 1) * 256].T)
        rows = slice(p * 256, (p + 1) * 256)
        base = front[:, N + p * 256 : N + (p + 1) * 256].T
        out[rows, :] = (base + zero[rows, :] + near[rows, :]) - mm3(h, w, uh, ul)


def body(child_front, child_order, parent_front, parent_order, row_map, col_map):
    sub = lax.axis_index("sub")
    prow = lax.axis_index("prow")
    pcol = lax.axis_index("pcol")
    front = child_front[0]
    parent_t = parent_front.T
    meta = jnp.stack([sub, pcol, prow]).astype(jnp.int32)

    piece, uppers, left_t = prep(front, parent_t)
    lows = [z_step(uppers, 1)]
    highs = [z_step(uppers, -1)]
    for _ in range(2):
        lows.append(z_step(lows[-1], 1))
        highs.append(z_step(highs[-1], -1))
    lows.append(z_step(lows[-1], 1))
    upper_parts = [uppers] + lows + highs

    pieces = lax.all_to_all(piece, "prow", 0, 0, tiled=True)
    left_parts = pcol_steps(left_t)
    ties = [left_parts[i] for i in (1, 2, 3, 4, 6, 7)] + [lows[0], highs[0]]
    (panel,) = call(
        mid_kernel, [sds(8, N + PP, PB)], [pieces] + ties, parts=len(ties)
    )
    panel = pcol_gather(panel)
    (parent_one,) = call(
        parent_rows_kernel,
        [sds(8 * PP, PB + PT)],
        [meta, panel] + left_parts,
        [pltpu.VMEM((8, PP, PB), F32), pltpu.VMEM((8, N, 256), F32), DMAS(9)],
        smem=1,
        parts=9,
    )
    parent_two = ylo_flip(parent_one)

    sh, sl, inv = call(
        child_inverse_kernel,
        [sds(PB, PB, dtype=BF16), sds(PB, PB, dtype=BF16), sds(PB, 1)],
        [meta, child_order, panel, parent_one, lows[2], highs[2]],
        [pltpu.VMEM((PB, PB), BF16)] * 2 + [pltpu.VMEM((PB, PB), F32)] * 2
        + [DMAS(8)],
        flops=SERIES_FLOPS,
        smem=1,
        parts=4,
    )
    own_lower, *terms = call(
        schur_kernel,
        [sds(N, CT)] + [sds(PT, 256)] * 4,
        [meta, row_map, col_map, child_order, inv]
        + left_parts
        + upper_parts
        + [sh, sl, front, parent_two],
        [pltpu.VMEM((PB, CT), F32)] * 3
        + [pltpu.VMEM((PB, PB), BF16)] * 2
        + [pltpu.VMEM((CT, CT + N), F32), DMAS(19)],
        flops=2 * PB * PB * CT * 6 + 2 * CT * PB * CT * 3,
        smem=3,
        parts=20,
    )
    over = core_flip(terms[3])
    near = core_flip(terms[1])
    far = ylo_flip(terms[2] + over)

    halves = [parent_one, parent_two, core_flip(parent_one), core_flip(parent_two)]
    parent_lower, partial = call(
        parent_kernel,
        [sds(PP, PT), sds(PT, 256)],
        [meta, parent_order[None]]
        + upper_parts
        + halves
        + [near, terms[0], parent_t],
        SERIES_SCRATCH
        + [pltpu.VMEM((PB, PB + PT), F32), pltpu.VMEM((PB, 256), F32)]
        + [pltpu.VMEM((PT, 256), F32)] * 2
        + [pltpu.VMEM((256, N + PT), F32), DMAS(15)],
        parts=15,
        moved=1024,
        flops=PB,
        smem=1,
    )
    return (own_lower.T[None], parent_lower.T, partial + far)


def solution(mesh):
    placed = (
        P("sub", "prow", "pcol"),
        P("sub", None),
        P("prow", ("sub", "pcol")),
        P(),
        P("sub", "prow"),
        P("sub", "pcol"),
    )
    return jax.shard_map(
        body,
        mesh=mesh,
        in_specs=placed,
        out_specs=(
            P("sub", "prow", "pcol"),
            P("prow", ("sub", "pcol")),
            P("prow", ("sub", "pcol")),
        ),
        check_vma=False,
    )
```

```python
import functools

import jax
import jax.numpy as jnp
from jax import lax
from jax.experimental import pallas as pl
from jax.experimental.pallas import tpu as pltpu
from jax.sharding import PartitionSpec as P

PB = 512
BLK = 128
N = 64
PP = 16
CT = 768
PT = 1024
F32 = jnp.float32
BF16 = jnp.bfloat16
VMEM = pl.BlockSpec(memory_space=pltpu.VMEM)
ANY = pl.BlockSpec(memory_space=pl.ANY)
HBM = pl.BlockSpec(memory_space=pltpu.HBM)
SMEM = pl.BlockSpec(memory_space=pltpu.SMEM)


def flip(axis, size, mask):
    return functools.partial(
        lax.ppermute, axis_name=axis, perm=[(i, i ^ mask) for i in range(size)]
    )


core_flip = flip("sub", 4, 1)
ylo_flip = flip("sub", 4, 2)
yhi_flip = flip("pcol", 8, 4)


def x_step(value, step):
    pairs = [(i, i // 4 * 4 + (i % 4 + step) % 4) for i in range(8)]
    return lax.ppermute(value, "pcol", pairs)


def pcol_gather(copies):
    return lax.all_to_all(copies, "pcol", 0, 0, tiled=True)


def pcol_steps(own):
    flip_own = yhi_flip(own)
    below, above = x_step(own, 1), x_step(own, -1)
    below_flip, above_flip = x_step(flip_own, 1), x_step(flip_own, -1)
    far, far_flip = x_step(below, 1), x_step(above_flip, -1)
    return [own, flip_own, below, below_flip, far, far_flip, above, above_flip]


def z_step(value, step):
    return lax.ppermute(value, "prow", [(i, (i + step) % 8) for i in range(8)])


def call(kernel, outs, ins, scratch=(), flops=0, smem=0, parts=0, moved=None, limit=60, where=ANY):
    whole = len(ins) - smem - parts
    if moved is None:
        moved = sum(o.size * o.dtype.itemsize for o in list(outs) + list(ins))
    return pl.pallas_call(
        kernel,
        out_shape=tuple(outs),
        in_specs=[SMEM] * smem + [VMEM] * whole + [where] * parts,
        out_specs=tuple([VMEM] * len(outs)),
        scratch_shapes=list(scratch),
        compiler_params=pltpu.CompilerParams(vmem_limit_bytes=limit * 1024 * 1024),
        cost_estimate=pl.CostEstimate(flops=flops, bytes_accessed=moved, transcendentals=0),
    )(*ins)


def sds(*shape, dtype=F32):
    return jax.ShapeDtypeStruct(shape, dtype)


def split(value):
    high = value.astype(BF16)
    return high, (value - high.astype(F32)).astype(BF16)


def mm(a, b):
    return jnp.dot(a, b, preferred_element_type=F32)


def mm3(ah, al, bh, bl):
    return mm(jnp.concatenate([ah, ah, al], 1), jnp.concatenate([bh, bl, bh], 0))


def select(hot, value):
    first = value.astype(BF16)
    rest = value - first.astype(F32)
    second = rest.astype(BF16)
    third = (rest - second.astype(F32)).astype(BF16)
    return mm(hot, first) + (mm(hot, second) + mm(hot, third))


def hot_rows(order, meta, held):
    sub, pcol = meta[0], meta[1]
    x, yhi = pcol & 3, pcol >> 2
    if held == "parent":
        owner = order >> 4
        pos = (((owner >> 3) ^ sub) & 1) * 2 + (((owner >> 4) ^ (sub >> 1)) & 1)
        pos = pos * 8 + ((x - owner) & 3) * 2 + (((owner >> 2) ^ yhi) & 1)
        pos = pos * PP + (order & (PP - 1))
    elif held == "left":
        owner = order >> 6
        pos = ((x - owner) & 3) * 2 * N + (((owner >> 2) ^ yhi) & 1) * N + (order & (N - 1))
    else:
        pos = order
    down = jnp.broadcast_to(pos.astype(F32), (BLK, PB)).T
    lanes = lax.broadcasted_iota(jnp.int32, (PB, BLK), 1)
    parts = []
    for c in range(PB // BLK):
        hit = down == (lanes + c * BLK).astype(F32)
        parts.append(jnp.where(hit, 1.0, 0.0).astype(BF16))
    return jnp.concatenate(parts, 1)


def series(panel_t, hot, ph, pw, th, tl, tf):
    eye = (
        lax.broadcasted_iota(jnp.int32, (PB, PB), 0) == lax.broadcasted_iota(jnp.int32, (PB, PB), 1)
    )
    picked = select(hot, panel_t)
    diag = jnp.sum(jnp.where(eye, picked, 0.0), axis=1, keepdims=True)
    inv_diag = 1.0 / diag
    error = jnp.where(eye, 1.0, 0.0) - picked * inv_diag
    ph[...], pw[...] = split(error)
    total = jnp.where(eye, 1.0, 0.0) + error
    tf[...] = total
    th[...], tl[...] = split(total)

    @pl.loop(0, 4)
    def _(_):
        h, w = split(mm3(ph[...], pw[...], ph[...], pw[...]))
        ph[...] = h
        pw[...] = w
        new = tf[...] + mm3(ph[...], pw[...], th[...], tl[...])
        tf[...] = new
        th[...], tl[...] = split(new)

    return inv_diag


SERIES_SCRATCH = [pltpu.VMEM((PB, PB), BF16)] * 4 + [pltpu.VMEM((PB, PB), F32)]
DMAS = lambda n: pltpu.SemaphoreType.DMA((n,))
SERIES_FLOPS = 2 * PB**3 * 27


def prep_kernel(front_rows, front_cols, parent_cols, parent_rows, piece, uppers, left_t):
    corner = front_rows[:, :N].T
    for z in range(8):
        piece[z, :32, :N] = corner[:32]
        piece[z, :32, N:] = corner[32:]
        piece[z, 32:, :N] = parent_cols[: PP // 2, :N]
        piece[z, 32:, N:] = parent_cols[PP // 2 : PP, :N]
    uppers[:, :CT] = front_rows[:, N:]
    uppers[:, CT:] = parent_cols[PP:, :N].T
    left_t[:, :CT] = front_cols[N:, :N].T
    for c in range(4):
        left_t[c * PP : (c + 1) * PP, CT:] = parent_rows[:, N + c * 256 : N + (c + 1) * 256]


def prep(front, parent_t):
    first = lambda i: (0, 0)
    return pl.pallas_call(
        prep_kernel,
        out_shape=(sds(8, 40, BLK), sds(N, PT), sds(N, CT + 256)),
        grid=(1,),
        in_specs=[
            pl.BlockSpec((N, CT + N), first),
            pl.BlockSpec((CT + N, BLK), first),
            pl.BlockSpec((PP + 256, BLK), first),
            pl.BlockSpec((PP, N + PT), first),
        ],
        out_specs=(
            pl.BlockSpec((8, 40, BLK), lambda i: (0, 0, 0)),
            pl.BlockSpec((N, PT), first),
            pl.BlockSpec((N, CT + 256), first),
        ),
        compiler_params=pltpu.CompilerParams(vmem_limit_bytes=60 * 1024 * 1024),
    )(front, front, parent_t, parent_t)


def mid_kernel(pieces, *refs):
    panel = refs[-1]
    for z in range(8):
        at = slice(z * N, (z + 1) * N)
        for i in range(8):
            panel[i, :32, at] = pieces[z, :32, :N]
            panel[i, 32:N, at] = pieces[z, :32, N:]
            panel[i, N : N + PP // 2, at] = pieces[z, 32:, :N]
            panel[i, N + PP // 2 :, at] = pieces[z, 32:, N:]


def x_fetch(dest, parts, sems):
    copies, start = [], 0
    for i, part in enumerate(parts):
        rows = pl.ds(start, part.shape[0])
        source = part.at[:, pl.ds(0, dest.shape[1])]
        copies.append(pltpu.make_async_copy(source, dest.at[rows, :], sems.at[i]))
        start += part.shape[0]
    return copies


def z_fetch(dest, cols, meta, parts, offset, sems):
    copies = []
    for i, part in enumerate(parts):
        owner = (meta[2] + (8 - i if i <= 4 else i - 4)) & 7
        rows = pl.ds(pl.multiple_of(owner * N, N), N)
        source = part.at[:, pl.ds(offset, cols)]
        copies.append(pltpu.make_async_copy(source, dest.at[rows, :], sems.at[i]))
    return copies


def begin(copies):
    for copy in copies:
        copy.start()


def finish(copies):
    for copy in copies:
        copy.wait()


def child_inverse_kernel(meta, order, blocks, *refs):
    sh, sl, inv, ph, pw, tf, panel, sems = refs[3:]
    copies = x_fetch(panel, [blocks.at[i, pl.ds(0, N), :] for i in range(8)], sems)
    begin(copies)
    hot = hot_rows(order[...], meta, "panel")
    finish(copies)
    inv[...] = series(panel[...], hot, ph, pw, sh, sl, tf)


def sources(targets, want):
    source, live = jnp.int32(0), jnp.int32(0)
    for j in range(6):
        hit = jnp.where(targets[j] == want, 1, 0).astype(jnp.int32)
        source += hit * j
        live += hit
    return source, live


def row_place(row_map, p):
    return sources([row_map[0, j] & 7 for j in range(6)], p)


def col_place(meta, col_map, q):
    values = [col_map[0, j] for j in range(6)]
    return sources([((v >> 4) ^ meta[0]) * 2 + (v & 1) for v in values], q)


def schur_kernel(meta, row_map, col_map, order, inv, *refs):
    left_parts, upper_parts, (sh_in, sl_in, front_in) = refs[:8], refs[8:16], refs[16:19]
    own_lower, outs = refs[20], refs[21:25]
    left, lower_t, upper, sh, sl, front, fetched = refs[25:]
    first = x_fetch(left, left_parts, fetched.at[pl.ds(0, 8)])
    second = [
        pltpu.make_async_copy(sh_in, sh, fetched.at[16]),
        pltpu.make_async_copy(sl_in, sl, fetched.at[17]),
    ]
    third = z_fetch(upper, CT, meta, upper_parts, 0, fetched.at[pl.ds(8, 8)])
    third.append(pltpu.make_async_copy(front_in.at[pl.ds(N, CT), :], front, fetched.at[18]))
    begin(first + second + third)
    hot = hot_rows(order[...], meta, "left")
    finish(first)
    high, low = split(select(hot, left[...]) * inv[...])
    finish(second)
    lower_t[...] = mm3(sh[...], sl[...], high, low)
    own_lower[...] = lower_t[pl.ds(pl.multiple_of(meta[1] * N, N), N), :]
    finish(third)
    uh, ul = split(upper[...])
    for i in range(3):
        lh, ll = split(lower_t[:, i * 256 : (i + 1) * 256].T)
        rows = slice(i * 256, (i + 1) * 256)
        front[rows, :CT] = front[rows, N:] - mm3(lh, ll, uh, ul)
    for slot, out in enumerate(outs):
        for b in range(2):
            csrc, clive = col_place(meta, col_map, slot * 2 + b)
            for p in range(8):
                rsrc, rlive = row_place(row_map, p)
                block = front[
                    pl.ds(pl.multiple_of(rsrc * BLK, BLK), BLK),
                    pl.ds(pl.multiple_of(csrc * BLK, BLK), BLK),
                ]
                here = (slice(p * BLK, (p + 1) * BLK), slice(b * BLK, (b + 1) * BLK))
                out[here] = jnp.where(rlive * clive > 0, block, 0.0)


def parent_rows_kernel(meta, blocks, *refs):
    parts, (out, panel, left, sems) = refs[:8], refs[8:]
    copies = [
        pltpu.make_async_copy(blocks.at[:, pl.ds(N, PP), :], panel, sems.at[8])
    ]
    for i, part in enumerate(parts):
        source = part.at[:, pl.ds(CT, 256)]
        copies.append(pltpu.make_async_copy(source, left.at[i], sems.at[i]))
    begin(copies)
    finish(copies)
    x, yhi = meta[1] & 3, meta[1] >> 2
    for i in range(8):
        owner = ((yhi ^ (i & 1)) * 4) + ((x - i // 2) & 3)
        rows = slice(i * PP, (i + 1) * PP)
        out[rows, :PB] = panel[owner]
        for c in range(4):
            at = slice(PB + c * 256, PB + (c + 1) * 256)
            out[rows, at] = left[i, c * PP : (c + 1) * PP, :]


def parent_kernel(meta, order, *refs):
    upper_parts, halves, tops, parent_t = refs[:8], refs[8:12], refs[12:14], refs[14]
    lower_out, out, ph, pw, th, tl, tf, whole, upper, near, zero, front, sems = refs[15:]
    first = x_fetch(whole, halves, sems.at[pl.ds(0, 4)])
    second = z_fetch(upper, 256, meta, upper_parts, CT, sems.at[pl.ds(4, 8)])
    second.append(pltpu.make_async_copy(tops[0], near, sems.at[12]))
    second.append(pltpu.make_async_copy(tops[1], zero, sems.at[13]))
    second.append(pltpu.make_async_copy(parent_t.at[pl.ds(PP, 256), :], front, sems.at[14]))
    begin(first + second)
    hot = hot_rows(order[...], meta, "parent")
    finish(first)
    inv = series(whole[:, :PB], hot, ph, pw, th, tl, tf)
    high, low = split(select(hot, whole[:, PB:]) * inv)
    whole[:, PB:] = mm3(th[...], tl[...], high, low)
    at = pl.multiple_of((meta[0] * 8 + meta[1]) * PP, PP)
    lower_out[...] = whole[pl.ds(at, PP), PB:]
    finish(second)
    uh, ul = split(upper[...])
    for p in range(4):
        h, w = split(whole[:, PB + p * 256 : PB + (p + 1) * 256].T)
        rows = slice(p * 256, (p + 1) * 256)
        base = front[:, N + p * 256 : N + (p + 1) * 256].T
        out[rows, :] = (base + zero[rows, :] + near[rows, :]) - mm3(h, w, uh, ul)


def body(child_front, child_order, parent_front, parent_order, row_map, col_map):
    sub = lax.axis_index("sub")
    prow = lax.axis_index("prow")
    pcol = lax.axis_index("pcol")
    front = child_front[0]
    parent_t = parent_front.T
    meta = jnp.stack([sub, pcol, prow]).astype(jnp.int32)

    piece, uppers, left_t = prep(front, parent_t)
    lows = [z_step(uppers, 1)]
    highs = [z_step(uppers, -1)]
    for _ in range(2):
        lows.append(z_step(lows[-1], 1))
        highs.append(z_step(highs[-1], -1))
    lows.append(z_step(lows[-1], 1))
    upper_parts = [uppers] + lows + highs

    pieces = lax.all_to_all(piece, "prow", 0, 0, tiled=True)
    left_parts = pcol_steps(left_t)
    ties = [left_parts[i] for i in (1, 2, 3, 4, 6, 7)]
    (panel,) = call(
        mid_kernel, [sds(8, N + PP, PB)], [pieces] + ties, parts=len(ties)
    )
    panel = pcol_gather(panel)
    (parent_one,) = call(
        parent_rows_kernel,
        [sds(8 * PP, PB + PT)],
        [meta, panel] + left_parts,
        [pltpu.VMEM((8, PP, PB), F32), pltpu.VMEM((8, N, 256), F32), DMAS(9)],
        smem=1,
        parts=9,
    )
    parent_two = ylo_flip(parent_one)

    sh, sl, inv = call(
        child_inverse_kernel,
        [sds(PB, PB, dtype=BF16), sds(PB, PB, dtype=BF16), sds(PB, 1)],
        [meta, child_order, panel, parent_one, lows[2], highs[2]],
        [pltpu.VMEM((PB, PB), BF16)] * 2 + [pltpu.VMEM((PB, PB), F32)] * 2
        + [DMAS(8)],
        flops=SERIES_FLOPS,
        smem=1,
        parts=4,
    )
    own_lower, *terms = call(
        schur_kernel,
        [sds(N, CT)] + [sds(PT, 256)] * 4,
        [meta, row_map, col_map, child_order, inv]
        + left_parts
        + upper_parts
        + [sh, sl, front, parent_two],
        [pltpu.VMEM((PB, CT), F32)] * 3
        + [pltpu.VMEM((PB, PB), BF16)] * 2
        + [pltpu.VMEM((CT, CT + N), F32), DMAS(19)],
        flops=2 * PB * PB * CT * 6 + 2 * CT * PB * CT * 3,
        smem=3,
        parts=20,
    )
    over = core_flip(terms[3])
    near = core_flip(terms[1])
    far = ylo_flip(terms[2] + over)

    halves = [parent_one, parent_two, core_flip(parent_one), core_flip(parent_two)]
    parent_lower, partial = call(
        parent_kernel,
        [sds(PP, PT), sds(PT, 256)],
        [meta, parent_order[None]]
        + upper_parts
        + halves
        + [near, terms[0], parent_t],
        SERIES_SCRATCH
        + [pltpu.VMEM((PB, PB + PT), F32), pltpu.VMEM((PB, 256), F32)]
        + [pltpu.VMEM((PT, 256), F32)] * 2
        + [pltpu.VMEM((256, N + PT), F32), DMAS(15)],
        parts=15,
        moved=1024,
        limit=40,
        where=HBM,
        flops=PB,
        smem=1,
    )
    return (own_lower.T[None], parent_lower.T, partial + far)


def solution(mesh):
    placed = (
        P("sub", "prow", "pcol"),
        P("sub", None),
        P("prow", ("sub", "pcol")),
        P(),
        P("sub", "prow"),
        P("sub", "pcol"),
    )
    return jax.shard_map(
        body,
        mesh=mesh,
        in_specs=placed,
        out_specs=(
            P("sub", "prow", "pcol"),
            P("prow", ("sub", "pcol")),
            P("prow", ("sub", "pcol")),
        ),
        check_vma=False,
    )
```

```python
import functools

import jax
import jax.numpy as jnp
from jax import lax
from jax.experimental import pallas as pl
from jax.experimental.pallas import tpu as pltpu
from jax.sharding import PartitionSpec as P

PB = 512
BLK = 128
N = 64
PP = 16
CT = 768
PT = 1024
F32 = jnp.float32
BF16 = jnp.bfloat16
VMEM = pl.BlockSpec(memory_space=pltpu.VMEM)
ANY = pl.BlockSpec(memory_space=pl.ANY)
HBM = pl.BlockSpec(memory_space=pltpu.HBM)
SMEM = pl.BlockSpec(memory_space=pltpu.SMEM)


def flip(axis, size, mask):
    return functools.partial(
        lax.ppermute, axis_name=axis, perm=[(i, i ^ mask) for i in range(size)]
    )


core_flip = flip("sub", 4, 1)
ylo_flip = flip("sub", 4, 2)
yhi_flip = flip("pcol", 8, 4)


def x_step(value, step):
    pairs = [(i, i // 4 * 4 + (i % 4 + step) % 4) for i in range(8)]
    return lax.ppermute(value, "pcol", pairs)


def pcol_gather(copies):
    return lax.all_to_all(copies, "pcol", 0, 0, tiled=True)


def pcol_steps(own):
    flip_own = yhi_flip(own)
    below, above = x_step(own, 1), x_step(own, -1)
    below_flip, above_flip = x_step(flip_own, 1), x_step(flip_own, -1)
    far, far_flip = x_step(below, 1), x_step(above_flip, -1)
    return [own, flip_own, below, below_flip, far, far_flip, above, above_flip]


def z_step(value, step):
    return lax.ppermute(value, "prow", [(i, (i + step) % 8) for i in range(8)])


def call(kernel, outs, ins, scratch=(), flops=0, smem=0, parts=0, moved=None, limit=60, where=ANY):
    whole = len(ins) - smem - parts
    if moved is None:
        moved = sum(o.size * o.dtype.itemsize for o in list(outs) + list(ins))
    return pl.pallas_call(
        kernel,
        out_shape=tuple(outs),
        in_specs=[SMEM] * smem + [VMEM] * whole + [where] * parts,
        out_specs=tuple([VMEM] * len(outs)),
        scratch_shapes=list(scratch),
        compiler_params=pltpu.CompilerParams(vmem_limit_bytes=limit * 1024 * 1024),
        cost_estimate=pl.CostEstimate(flops=flops, bytes_accessed=moved, transcendentals=0),
    )(*ins)


def sds(*shape, dtype=F32):
    return jax.ShapeDtypeStruct(shape, dtype)


def split(value):
    high = value.astype(BF16)
    return high, (value - high.astype(F32)).astype(BF16)


def mm(a, b):
    return jnp.dot(a, b, preferred_element_type=F32)


def mm3(ah, al, bh, bl):
    return mm(jnp.concatenate([ah, ah, al], 1), jnp.concatenate([bh, bl, bh], 0))


def select(hot, value):
    first = value.astype(BF16)
    rest = value - first.astype(F32)
    second = rest.astype(BF16)
    third = (rest - second.astype(F32)).astype(BF16)
    return mm(jnp.concatenate([hot, hot, hot], 1), jnp.concatenate([first, second, third], 0))


def hot_rows(order, meta, held):
    sub, pcol = meta[0], meta[1]
    x, yhi = pcol & 3, pcol >> 2
    if held == "parent":
        owner = order >> 4
        pos = (((owner >> 3) ^ sub) & 1) * 2 + (((owner >> 4) ^ (sub >> 1)) & 1)
        pos = pos * 8 + ((x - owner) & 3) * 2 + (((owner >> 2) ^ yhi) & 1)
        pos = pos * PP + (order & (PP - 1))
    elif held == "left":
        owner = order >> 6
        pos = ((x - owner) & 3) * 2 * N + (((owner >> 2) ^ yhi) & 1) * N + (order & (N - 1))
    else:
        pos = order
    down = jnp.broadcast_to(pos.astype(F32), (BLK, PB)).T
    lanes = lax.broadcasted_iota(jnp.int32, (PB, BLK), 1)
    parts = []
    for c in range(PB // BLK):
        hit = down == (lanes + c * BLK).astype(F32)
        parts.append(jnp.where(hit, 1.0, 0.0).astype(BF16))
    return jnp.concatenate(parts, 1)


def series(panel_t, hot, ph, pw, th, tl, tf):
    eye = (
        lax.broadcasted_iota(jnp.int32, (PB, PB), 0) == lax.broadcasted_iota(jnp.int32, (PB, PB), 1)
    )
    picked = select(hot, panel_t)
    diag = jnp.sum(jnp.where(eye, picked, 0.0), axis=1, keepdims=True)
    inv_diag = 1.0 / diag
    error = jnp.where(eye, 1.0, 0.0) - picked * inv_diag
    ph[...], pw[...] = split(error)
    total = jnp.where(eye, 1.0, 0.0) + error
    tf[...] = total
    th[...], tl[...] = split(total)

    ph[...], pw[...] = split(mm3(ph[...], pw[...], ph[...], pw[...]))

    @pl.loop(0, 3)
    def _(_):
        high = jnp.concatenate([ph[...], th[...]], 1)
        low = jnp.concatenate([pw[...], tl[...]], 1)
        both = mm3(ph[...], pw[...], high, low)
        ph[...], pw[...] = split(both[:, :PB])
        new = tf[...] + both[:, PB:]
        tf[...] = new
        th[...], tl[...] = split(new)

    th[...], tl[...] = split(tf[...] + mm3(ph[...], pw[...], th[...], tl[...]))
    return inv_diag


SERIES_SCRATCH = [pltpu.VMEM((PB, PB), BF16)] * 4 + [pltpu.VMEM((PB, PB), F32)]
DMAS = lambda n: pltpu.SemaphoreType.DMA((n,))
SERIES_FLOPS = 2 * PB**3 * 27


def prep_kernel(front_rows, front_cols, parent_cols, parent_rows, piece, uppers, left_t):
    corner = front_rows[:, :N].T
    for z in range(8):
        piece[z, :32, :N] = corner[:32]
        piece[z, :32, N:] = corner[32:]
        piece[z, 32:, :N] = parent_cols[: PP // 2, :N]
        piece[z, 32:, N:] = parent_cols[PP // 2 : PP, :N]
    uppers[:, :CT] = front_rows[:, N:]
    uppers[:, CT:] = parent_cols[PP:, :N].T
    left_t[:, :CT] = front_cols[N:, :N].T
    for c in range(4):
        left_t[c * PP : (c + 1) * PP, CT:] = parent_rows[:, N + c * 256 : N + (c + 1) * 256]


def prep(front, parent_t):
    first = lambda i: (0, 0)
    return pl.pallas_call(
        prep_kernel,
        out_shape=(sds(8, 40, BLK), sds(N, PT), sds(N, CT + 256)),
        grid=(1,),
        in_specs=[
            pl.BlockSpec((N, CT + N), first),
            pl.BlockSpec((CT + N, BLK), first),
            pl.BlockSpec((PP + 256, BLK), first),
            pl.BlockSpec((PP, N + PT), first),
        ],
        out_specs=(
            pl.BlockSpec((8, 40, BLK), lambda i: (0, 0, 0)),
            pl.BlockSpec((N, PT), first),
            pl.BlockSpec((N, CT + 256), first),
        ),
        compiler_params=pltpu.CompilerParams(vmem_limit_bytes=60 * 1024 * 1024),
    )(front, front, parent_t, parent_t)


def mid_kernel(pieces, *refs):
    panel = refs[-1]
    for z in range(8):
        at = slice(z * N, (z + 1) * N)
        for i in range(8):
            panel[i, :32, at] = pieces[z, :32, :N]
            panel[i, 32:N, at] = pieces[z, :32, N:]
            panel[i, N : N + PP // 2, at] = pieces[z, 32:, :N]
            panel[i, N + PP // 2 :, at] = pieces[z, 32:, N:]


def x_fetch(dest, parts, sems):
    copies, start = [], 0
    for i, part in enumerate(parts):
        rows = pl.ds(start, part.shape[0])
        source = part.at[:, pl.ds(0, dest.shape[1])]
        copies.append(pltpu.make_async_copy(source, dest.at[rows, :], sems.at[i]))
        start += part.shape[0]
    return copies


def z_fetch(dest, cols, meta, parts, offset, sems):
    copies = []
    for i, part in enumerate(parts):
        owner = (meta[2] + (8 - i if i <= 4 else i - 4)) & 7
        rows = pl.ds(pl.multiple_of(owner * N, N), N)
        source = part.at[:, pl.ds(offset, cols)]
        copies.append(pltpu.make_async_copy(source, dest.at[rows, :], sems.at[i]))
    return copies


def begin(copies):
    for copy in copies:
        copy.start()


def finish(copies):
    for copy in copies:
        copy.wait()


def child_inverse_kernel(meta, order, blocks, *refs):
    sh, sl, inv, ph, pw, tf, panel, sems = refs[3:]
    copies = x_fetch(panel, [blocks.at[i, pl.ds(0, N), :] for i in range(8)], sems)
    begin(copies)
    hot = hot_rows(order[...], meta, "panel")
    finish(copies)
    inv[...] = series(panel[...], hot, ph, pw, sh, sl, tf)


def sources(targets, want):
    source, live = jnp.int32(0), jnp.int32(0)
    for j in range(6):
        hit = jnp.where(targets[j] == want, 1, 0).astype(jnp.int32)
        source += hit * j
        live += hit
    return source, live


def row_place(row_map, p):
    return sources([row_map[0, j] & 7 for j in range(6)], p)


def col_place(meta, col_map, q):
    values = [col_map[0, j] for j in range(6)]
    return sources([((v >> 4) ^ meta[0]) * 2 + (v & 1) for v in values], q)


def schur_kernel(meta, row_map, col_map, order, inv, *refs):
    left_parts, upper_parts, (sh_in, sl_in, front_in) = refs[:8], refs[8:16], refs[16:19]
    own_lower, outs = refs[20], refs[21:25]
    left, lower_t, upper, sh, sl, front, fetched = refs[25:]
    first = x_fetch(left, left_parts, fetched.at[pl.ds(0, 8)])
    second = [
        pltpu.make_async_copy(sh_in, sh, fetched.at[16]),
        pltpu.make_async_copy(sl_in, sl, fetched.at[17]),
    ]
    third = z_fetch(upper, CT, meta, upper_parts, 0, fetched.at[pl.ds(8, 8)])
    third.append(pltpu.make_async_copy(front_in.at[pl.ds(N, CT), :], front, fetched.at[18]))
    begin(first + second + third)
    hot = hot_rows(order[...], meta, "left")
    finish(first)
    high, low = split(select(hot, left[...]) * inv[...])
    finish(second)
    lower_t[...] = mm3(sh[...], sl[...], high, low)
    own_lower[...] = lower_t[pl.ds(pl.multiple_of(meta[1] * N, N), N), :]
    finish(third)
    uh, ul = split(upper[...])
    for i in range(3):
        lh, ll = split(lower_t[:, i * 256 : (i + 1) * 256].T)
        rows = slice(i * 256, (i + 1) * 256)
        front[rows, :CT] = front[rows, N:] - mm3(lh, ll, uh, ul)
    for slot, out in enumerate(outs):
        for b in range(2):
            csrc, clive = col_place(meta, col_map, slot * 2 + b)
            for p in range(8):
                rsrc, rlive = row_place(row_map, p)
                block = front[
                    pl.ds(pl.multiple_of(rsrc * BLK, BLK), BLK),
                    pl.ds(pl.multiple_of(csrc * BLK, BLK), BLK),
                ]
                here = (slice(p * BLK, (p + 1) * BLK), slice(b * BLK, (b + 1) * BLK))
                out[here] = jnp.where(rlive * clive > 0, block, 0.0)


def parent_rows_kernel(meta, blocks, *refs):
    parts, (out, panel, left, sems) = refs[:8], refs[8:]
    copies = [
        pltpu.make_async_copy(blocks.at[:, pl.ds(N, PP), :], panel, sems.at[8])
    ]
    for i, part in enumerate(parts):
        source = part.at[:, pl.ds(CT, 256)]
        copies.append(pltpu.make_async_copy(source, left.at[i], sems.at[i]))
    begin(copies)
    finish(copies)
    x, yhi = meta[1] & 3, meta[1] >> 2
    for i in range(8):
        owner = ((yhi ^ (i & 1)) * 4) + ((x - i // 2) & 3)
        rows = slice(i * PP, (i + 1) * PP)
        out[rows, :PB] = panel[owner]
        for c in range(4):
            at = slice(PB + c * 256, PB + (c + 1) * 256)
            out[rows, at] = left[i, c * PP : (c + 1) * PP, :]


def parent_kernel(meta, order, *refs):
    upper_parts, halves, tops, parent_t = refs[:8], refs[8:12], refs[12:14], refs[14]
    lower_out, out, ph, pw, th, tl, tf, whole, upper, near, zero, front, sems = refs[15:]
    first = x_fetch(whole, halves, sems.at[pl.ds(0, 4)])
    second = z_fetch(upper, 256, meta, upper_parts, CT, sems.at[pl.ds(4, 8)])
    second.append(pltpu.make_async_copy(tops[0], near, sems.at[12]))
    second.append(pltpu.make_async_copy(tops[1], zero, sems.at[13]))
    second.append(pltpu.make_async_copy(parent_t.at[pl.ds(PP, 256), :], front, sems.at[14]))
    begin(first + second)
    hot = hot_rows(order[...], meta, "parent")
    finish(first)
    inv = series(whole[:, :PB], hot, ph, pw, th, tl, tf)
    high, low = split(select(hot, whole[:, PB:]) * inv)
    whole[:, PB:] = mm3(th[...], tl[...], high, low)
    at = pl.multiple_of((meta[0] * 8 + meta[1]) * PP, PP)
    lower_out[...] = whole[pl.ds(at, PP), PB:]
    finish(second)
    uh, ul = split(upper[...])
    for p in range(4):
        h, w = split(whole[:, PB + p * 256 : PB + (p + 1) * 256].T)
        rows = slice(p * 256, (p + 1) * 256)
        base = front[:, N + p * 256 : N + (p + 1) * 256].T
        out[rows, :] = (base + zero[rows, :] + near[rows, :]) - mm3(h, w, uh, ul)


def body(child_front, child_order, parent_front, parent_order, row_map, col_map):
    sub = lax.axis_index("sub")
    prow = lax.axis_index("prow")
    pcol = lax.axis_index("pcol")
    front = child_front[0]
    parent_t = parent_front.T
    meta = jnp.stack([sub, pcol, prow]).astype(jnp.int32)

    piece, uppers, left_t = prep(front, parent_t)
    lows = [z_step(uppers, 1)]
    highs = [z_step(uppers, -1)]
    for _ in range(2):
        lows.append(z_step(lows[-1], 1))
        highs.append(z_step(highs[-1], -1))
    lows.append(z_step(lows[-1], 1))
    upper_parts = [uppers] + lows + highs

    pieces = lax.all_to_all(piece, "prow", 0, 0, tiled=True)
    left_parts = pcol_steps(left_t)
    ties = [left_parts[i] for i in (1, 2, 3, 4, 6, 7)]
    (panel,) = call(
        mid_kernel,
        [sds(8, N + PP, PB)],
        [pieces] + ties,
        parts=len(ties),
        limit=16,
        where=HBM,
    )
    panel = pcol_gather(panel)
    (parent_one,) = call(
        parent_rows_kernel,
        [sds(8 * PP, PB + PT)],
        [meta, panel] + left_parts,
        [pltpu.VMEM((8, PP, PB), F32), pltpu.VMEM((8, N, 256), F32), DMAS(9)],
        smem=1,
        parts=9,
    )
    parent_two = ylo_flip(parent_one)

    sh, sl, inv = call(
        child_inverse_kernel,
        [sds(PB, PB, dtype=BF16), sds(PB, PB, dtype=BF16), sds(PB, 1)],
        [meta, child_order, panel, parent_one, lows[2], highs[2]],
        [pltpu.VMEM((PB, PB), BF16)] * 2 + [pltpu.VMEM((PB, PB), F32)] * 2
        + [DMAS(8)],
        flops=SERIES_FLOPS,
        smem=1,
        parts=4,
    )
    own_lower, *terms = call(
        schur_kernel,
        [sds(N, CT)] + [sds(PT, 256)] * 4,
        [meta, row_map, col_map, child_order, inv]
        + left_parts
        + upper_parts
        + [sh, sl, front, parent_two],
        [pltpu.VMEM((PB, CT), F32)] * 3
        + [pltpu.VMEM((PB, PB), BF16)] * 2
        + [pltpu.VMEM((CT, CT + N), F32), DMAS(19)],
        flops=2 * PB * PB * CT * 6 + 2 * CT * PB * CT * 3,
        smem=3,
        parts=20,
    )
    over = core_flip(terms[3])
    near = core_flip(terms[1])
    far = ylo_flip(terms[2] + over)

    halves = [parent_one, parent_two, core_flip(parent_one), core_flip(parent_two)]
    parent_lower, partial = call(
        parent_kernel,
        [sds(PP, PT), sds(PT, 256)],
        [meta, parent_order[None]]
        + upper_parts
        + halves
        + [near, terms[0], parent_t],
        SERIES_SCRATCH
        + [pltpu.VMEM((PB, PB + PT), F32), pltpu.VMEM((PB, 256), F32)]
        + [pltpu.VMEM((PT, 256), F32)] * 2
        + [pltpu.VMEM((256, N + PT), F32), DMAS(15)],
        parts=15,
        moved=1024,
        limit=40,
        where=HBM,
        flops=PB,
        smem=1,
    )
    return (own_lower.T[None], parent_lower.T, partial + far)


def solution(mesh):
    placed = (
        P("sub", "prow", "pcol"),
        P("sub", None),
        P("prow", ("sub", "pcol")),
        P(),
        P("sub", "prow"),
        P("sub", "pcol"),
    )
    return jax.shard_map(
        body,
        mesh=mesh,
        in_specs=placed,
        out_specs=(
            P("sub", "prow", "pcol"),
            P("prow", ("sub", "pcol")),
            P("prow", ("sub", "pcol")),
        ),
        check_vma=False,
    )
```
